32 devices in a mesh: lat: 8 (over z, y), lon: 4 (over x, core).
Axes of the slice: x: 2, y: 2, z: 4, core: 2. Of those that a mesh axis runs over, the one named last changes fastest.
Arguments:
- grid_in: float32 [8192, 512], P(('lat', 'lon')), may hold values from -6 to 6
- target: float32 [8192, 128], P(('lat', 'lon')), may hold values from -6 to 6
- w_enc: float32 [512, 512], replicated, may hold values from -0.25 to 0.25
- w_mix_self: float32 [2, 512, 512], replicated, may hold values from -0.25 to 0.25
- w_mix_nbr: float32 [2, 512, 512], replicated, may hold values from -0.25 to 0.25
- w_dec: float32 [512, 512], replicated, may hold values from -0.25 to 0.25
- w_out: float32 [512, 128], replicated, may hold values from -0.25 to 0.25
- var_weight: int32 [128], replicated, may hold values from 1 to 8
- g2m_idx: int32 [1024, 8], P(('lat', 'lon')), may hold values from 0 to 511, as said below
- g2m_w: float32 [1024, 8], P(('lat', 'lon')), may hold values from 0.1 to 1
- mesh_nbr: int32 [1024, 6], P(('lat', 'lon')), may hold values from 0 to 1023, as said below
- m2g_idx: int32 [8192, 4], P(('lat', 'lon')), may hold values from 0 to 1023, as said below
- m2g_w: float32 [8192, 4], P(('lat', 'lon')), may hold values from 0.1 to 1
Outputs:
- pred: float32 [8192, 128], P(('lat', 'lon'))
- loss: float32 [], replicated
- grad_out: float32 [512, 128], replicated
The draws below stay inside these ranges and needn't reach their ends.
Inputs may be any that keep to these rules, and one draw needn't show every extreme that they name: `g2m_idx`: an entry of row r names a block held by a device whose lat index differs by at most one from that of the device holding row r, and whose lon index differs by at most one, counted cyclically over the 4 tiles; blocks of device d are rows d * 16 onward. `mesh_nbr`: an entry of row r names a mesh node held by a device whose lat index differs by at most one from that of the device holding row r, and whose lon index differs by at most one, counted cyclically over the 4 tiles. `m2g_idx`: an entry of row r names a mesh node held by a device whose lat index differs by at most one from that of the device holding row r, and whose lon index differs by at most one, counted cyclically over the 4 tiles.
All inputs are finite; a program needn't handle non-finite values.
Results may differ from the reference program's by a relative error of at most 0.00028.
Values sent between devices are 32-bit elements; how exact they have to be, the bound alone decides.
No kernel may reach another device: no remote copies, remote signals or barrier semaphores. Data moves between devices by JAX's collectives and lax.ppermute only.
A program may use at most 64 MiB of HBM per device.

```python
import jax
import jax.numpy as jnp
from jax import lax

D = 512
V = 128
BS = 16
K = 8
K2 = 4
E = 6
L = 2
G_DEV = 256
MESH_DEV = 32
GRID = 8192
MESH = 1024
N_LAT = 8
N_LON = 4


def local_rows(key, rows, per_dev, source_dev, width):
    device = jnp.arange(rows, dtype=jnp.int32) // per_dev
    band = device // N_LON
    tile = device % N_LON
    key_a, key_b, key_c = jax.random.split(key, 3)
    offset = jax.random.randint(key_a, (rows, width), -1, 2, dtype=jnp.int32)
    src_band = jnp.clip(band[:, None] + offset, 0, N_LAT - 1)
    pick = jax.random.randint(key_b, (rows, width), 0, 5, dtype=jnp.int32)
    step = jnp.where(pick == 3, -1, jnp.where(pick == 4, 1, 0)).astype(jnp.int32)
    src_tile = (tile[:, None] + step + N_LON) % N_LON
    src_row = jax.random.randint(key_c, (rows, width), 0, source_dev, dtype=jnp.int32)
    return ((src_band * N_LON + src_tile) * source_dev + src_row).astype(jnp.int32)


def draw_g2m_idx(key, part):
    return local_rows(jax.random.fold_in(key, 11), MESH, MESH_DEV, G_DEV // BS, K)


def draw_mesh_nbr(key, part):
    return local_rows(jax.random.fold_in(key, 23), MESH, MESH_DEV, MESH_DEV, E)


def draw_m2g_idx(key, part):
    return local_rows(jax.random.fold_in(key, 37), GRID, G_DEV, MESH_DEV, K2)


def with_ends(values, key, smallest, high):
    longest = values.shape.index(max(values.shape))
    spots = []
    for shift in (0, 1):
        where = [jax.random.randint(jax.random.fold_in(key, axis), (), 0, length) for axis, length in enumerate(values.shape)]
        where[longest] = (where[longest] + shift) % values.shape[longest]
        spots.append(tuple(where))
    return values.at[spots[0]].set(smallest).at[spots[1]].set(high)


def level_of(own_key, shape, cuts, least, high):
    def one(dim, parts):
        heights = jax.random.uniform(jax.random.fold_in(jax.random.fold_in(own_key, 6), dim), (parts,), jnp.float32, least / len(cuts), high / len(cuts))
        return jnp.repeat(jnp.exp(heights), shape[dim] // parts).reshape((-1,) + (1,) * (len(shape) - dim - 1))

    factor_of = one(*cuts[0])
    for cut in cuts[1:]:
        factor_of = factor_of * one(*cut)
    return factor_of


def bell_draw(key, dims, scale, most, pieces=(), held_as=jnp.bfloat16):
    array = jax.random.normal(key, dims, jnp.float32) * scale
    if len(pieces) > 0:
        array = level_of(key, dims, pieces, -0.22, 0.18) * array
    return jnp.clip(array, min=-most, max=most).astype(held_as)


def setup_inputs(seed: int = 0) -> dict:
    keys = jax.random.split(jax.random.key(seed), 14)
    return {
        "grid_in": bell_draw(keys[0], (GRID, D), 1.0, 6.0, ((0, 32),), jnp.float32),
        "target": bell_draw(keys[1], (GRID, V), 1.0, 6.0, ((0, 32),), jnp.float32),
        "w_enc": bell_draw(keys[2], (D, D), D ** -0.5, 0.25, (), jnp.float32),
        "w_mix_self": bell_draw(keys[3], (L, D, D), D ** -0.5, 0.25, (), jnp.float32),
        "w_mix_nbr": bell_draw(keys[4], (L, D, D), D ** -0.5, 0.25, (), jnp.float32),
        "w_dec": bell_draw(keys[5], (D, D), D ** -0.5, 0.25, (), jnp.float32),
        "w_out": bell_draw(keys[6], (D, V), D ** -0.5, 0.25, (), jnp.float32),
        "var_weight": with_ends(jax.random.randint(keys[7], (V,), 1, 9), jax.random.fold_in(keys[7], 1), 1, 8).astype(jnp.int32),
        "g2m_idx": draw_g2m_idx(jax.random.fold_in(keys[13], 71), 0),
        "g2m_w": jnp.clip(0.1 + 0.9 * jax.random.uniform(keys[9], (MESH, K), jnp.float32) ** level_of(keys[9], (MESH, K), ((0, 32),), -0.2, 0.2), 0.1, 1.0),
        "mesh_nbr": draw_mesh_nbr(jax.random.fold_in(keys[13], 71), 0),
        "m2g_idx": draw_m2g_idx(jax.random.fold_in(keys[13], 71), 0),
        "m2g_w": jnp.clip(0.1 + 0.9 * jax.random.uniform(keys[12], (GRID, K2), jnp.float32) ** level_of(keys[12], (GRID, K2), ((0, 32),), -0.2, 0.2), 0.1, 1.0),
    }


def silu(value):
    return value / (1.0 + jnp.exp(-value))

def matmul(left, right):
    return jnp.dot(left, right, precision=lax.Precision.HIGHEST, preferred_element_type=jnp.float32)

def interp(table, index, weights):
    total = jnp.zeros((index.shape[0], table.shape[1]), jnp.float32)
    for slot in range(index.shape[1]):
        total = total + weights[:, slot:slot + 1] * jnp.take(table, index[:, slot], axis=0)
    return total / lax.optimization_barrier(jnp.sum(weights, axis=1, keepdims=True))

def mixing(mesh, mesh_nbr, self_weight, nbr_weight):
    agg = jnp.zeros_like(mesh)
    for slot in range(mesh_nbr.shape[1]):
        agg = agg + jnp.take(mesh, mesh_nbr[:, slot], axis=0)
    agg = agg / mesh_nbr.shape[1]
    center = mesh - lax.optimization_barrier(jnp.mean(mesh, axis=1, keepdims=True))
    nrm = center / jnp.sqrt(lax.optimization_barrier(jnp.mean(center * center, axis=1, keepdims=True)) + 1e-05)
    return mesh + silu(matmul(nrm, self_weight) + matmul(agg, nbr_weight))

def reference(grid_in, target, w_enc, w_mix_self, w_mix_nbr, w_dec, w_out, var_weight, g2m_idx, g2m_w, mesh_nbr, m2g_idx, m2g_w):
    h_one = grid_in + silu(matmul(grid_in, w_enc))
    blocks = lax.optimization_barrier(jnp.mean(h_one.reshape(-1, BS, D), axis=1))
    mesh = interp(blocks, g2m_idx, g2m_w)
    for layer in range(L):
        mesh = mixing(mesh, mesh_nbr, w_mix_self[layer], w_mix_nbr[layer])
    back = interp(mesh, m2g_idx, m2g_w)
    hidden = silu(matmul(h_one + back, w_dec))
    pred = matmul(hidden, w_out)
    scale = lax.optimization_barrier(jnp.sum(target * target, axis=0)) / GRID + 1e-06
    resid = pred - target
    err = lax.optimization_barrier(jnp.sum(resid * resid, axis=0))
    weights = var_weight.astype(jnp.float32)
    wsum = jnp.sum(weights)
    loss = jnp.sum(weights * err / (scale * GRID * wsum))
    coef = 2.0 * weights / (scale * GRID * wsum)
    grad_out = matmul(hidden.T, resid) * coef[None, :]
    return (pred, loss, grad_out)
```

```python
import functools

import jax
import jax.numpy as jnp
from jax import lax
from jax.experimental import pallas as pl
from jax.experimental.pallas import tpu as pltpu
from jax.sharding import PartitionSpec as P

BS = 16
L = 2
AXES = ("lat", "lon")
F32 = jnp.float32
BF16 = jnp.bfloat16
LANES = 128
GROUP = 32
TILE = 128
VMEM_LIMIT = 56 * 1024 * 1024


def split(value):
    high = value.astype(BF16)
    return high, (value - high.astype(F32)).astype(BF16)


def dot(left, right):
    return jnp.dot(left, right, preferred_element_type=F32)


def dot3(left, right):
    (lh, ll), (rh, rl) = left, right
    return dot(lh, rh) + (dot(lh, rl) + dot(ll, rh))


def silu(value):
    return value / (1.0 + jnp.exp(-value))


def vmem():
    return pl.BlockSpec(memory_space=pltpu.VMEM)


def smem():
    return pl.BlockSpec(memory_space=pltpu.SMEM)


def shape(dims, dtype=F32):
    return jax.ShapeDtypeStruct(dims, dtype)


def encode_kernel(x_ref, w_ref, e_ref, h_ref, p_ref):
    x = x_ref[...]
    h = x + silu(dot3(split(x), split(w_ref[...])))
    h_ref[...] = h
    rows, width = x.shape
    n_blocks = rows // BS
    means = jnp.sum(h.reshape(n_blocks, BS, width), axis=1) * (1.0 / BS)
    for part in range(n_blocks // 8):
        p_ref[:, part * width:(part + 1) * width] = means[part * 8:(part + 1) * 8]
    p_ref[:, (n_blocks // 8) * width:] = e_ref[...]


def prepare_kernel(base_node, s_ref, ws_ref, wn_ref, wd_ref, wo_ref, i_ref, c_ref, wh_ref, wl_ref, oh_ref, ol_ref, ah_ref, al_ref):
    for layer in range(L):
        wh_ref[2 * layer], wl_ref[2 * layer] = split(ws_ref[layer])
        wh_ref[2 * layer + 1], wl_ref[2 * layer + 1] = split(wn_ref[layer])
    wh_ref[2 * L], wl_ref[2 * L] = split(wd_ref[...])
    oh_ref[...], ol_ref[...] = split(wo_ref[...])
    rows, nodes = ah_ref.shape
    spread = i_ref.shape[1]
    local = (i_ref[...] - s_ref[4] * base_node).astype(F32)
    coef = c_ref[...]
    coef = coef / jnp.sum(coef, axis=1, keepdims=True)
    step = 32
    column = lax.broadcasted_iota(jnp.int32, (step, nodes), 1).astype(F32)
    for at in range(0, rows, step):
        total = jnp.zeros((step, nodes), F32)
        for k in range(spread):
            total = total + jnp.where(column == local[at:at + step, k:k + 1], coef[at:at + step, k:k + 1], 0.0)
        ah_ref[at:at + step], al_ref[at:at + step] = split(total)


def mesh_kernel(plan, s_ref, *refs):
    n_tables = plan["tables"]
    tables, refs = refs[:n_tables], refs[n_tables:]
    (wh_ref, wl_ref, oh_ref, ol_ref, ah_ref, al_ref, h_ref, t_ref, pred_ref, keep_ref, send_ref,
     th, tl, info, m0f, m0h, m0l, m1f, m1h, m1l, m2h, m2l) = refs
    width = h_ref.shape[1]
    lon, n_blocks, nodes = plan["lon"], plan["blocks"], plan["nodes"]
    k_g2m, k_nbr = plan["k_g2m"], plan["k_nbr"]
    slots = tables[0].shape[0]
    me = s_ref[0]
    for c, table in enumerate(tables):
        for i in range(slots):
            if plan["xor"] is None:
                place = i
            else:
                place = me ^ plan["xor"][c * slots + i]
            tile = table[i]
            rows = jnp.concatenate([tile[:, p * width:(p + 1) * width] for p in range(n_blocks // 8)], axis=0)
            at = pl.multiple_of(place * n_blocks, n_blocks)
            th[pl.ds(at, n_blocks), :], tl[pl.ds(at, n_blocks), :] = split(rows)
            info[place] = tile[:, (n_blocks // 8) * width:]

    per_step = TILE // nodes
    groups = nodes // 8

    def node_rows(first, build):
        out = []
        for d in range(per_step):
            tile = info[first + d]
            for j in range(groups):
                out.append(build(tile, j * GROUP))
        return out

    first0 = (s_ref[2] - s_ref[1]) * lon
    base_block = (s_ref[1] * (lon * n_blocks)).astype(F32)
    column_b = lax.broadcasted_iota(jnp.int32, (8, th.shape[0]), 1).astype(F32)

    def to_mesh(step, carry):
        def build(tile, lane):
            local = tile - base_block
            total = jnp.zeros(column_b.shape, F32)
            norm = jnp.zeros((8, 1), F32)
            for k in range(k_g2m):
                coef = tile[:, lane + k_g2m + k:lane + k_g2m + k + 1]
                total = total + jnp.where(column_b == local[:, lane + k:lane + k + 1], coef, 0.0)
                norm = norm + coef
            return total, jnp.where(norm == 0.0, 1.0, norm)

        parts = node_rows(first0 + step * per_step, build)
        matrix = jnp.concatenate([p[0] for p in parts], axis=0)
        norm = jnp.concatenate([p[1] for p in parts], axis=0)
        value = dot3(split(matrix), (th[...], tl[...])) / norm
        at = pl.ds(pl.multiple_of(step * TILE, TILE), TILE)
        m0f[at, :] = value
        m0h[at, :], m0l[at, :] = split(value)
        return carry

    lax.fori_loop(0, m0f.shape[0] // TILE, to_mesh, 0)

    def mixing(layer, src, src_band, out, out_band):
        srcf, srch, srcl = src
        column = lax.broadcasted_iota(jnp.int32, (8, srch.shape[0]), 1).astype(F32)
        base = (src_band * (lon * nodes)).astype(F32)
        first = (out_band - s_ref[1]) * lon
        shift = (out_band - src_band) * (lon * nodes)
        self_weight = (wh_ref[2 * layer], wl_ref[2 * layer])
        nbr_weight = (wh_ref[2 * layer + 1], wl_ref[2 * layer + 1])

        def body(step, carry):
            def build(tile, lane):
                local = tile - base
                total = jnp.zeros(column.shape, F32)
                for k in range(k_nbr):
                    at = lane + 2 * k_g2m + k
                    total = total + jnp.where(column == local[:, at:at + 1], 1.0, 0.0)
                return total

            matrix = jnp.concatenate(node_rows(first + step * per_step, build), axis=0).astype(BF16)
            agg = (dot(matrix, srch[...]) + dot(matrix, srcl[...])) * (1.0 / k_nbr)
            own = srcf[pl.ds(pl.multiple_of(shift + step * TILE, nodes), TILE), :]
            center = own - jnp.mean(own, axis=1, keepdims=True)
            nrm = center / jnp.sqrt(jnp.mean(center * center, axis=1, keepdims=True) + 1e-05)
            value = own + silu(dot3(split(nrm), self_weight) + dot3(split(agg), nbr_weight))
            at = pl.ds(pl.multiple_of(step * TILE, TILE), TILE)
            if out[0] is not None:
                out[0][at, :] = value
            out[1][at, :], out[2][at, :] = split(value)
            return carry

        lax.fori_loop(0, out[1].shape[0] // TILE, body, 0)

    mixing(0, (m0f, m0h, m0l), s_ref[2], (m1f, m1h, m1l), s_ref[3])
    mixing(1, (m1f, m1h, m1l), s_ref[3], (None, m2h, m2l), s_ref[4])

    x = h_ref[...] + dot3((ah_ref[...], al_ref[...]), (m2h[...], m2l[...]))
    z = split(silu(dot3(split(x), (wh_ref[2 * L], wl_ref[2 * L]))))
    pred = dot3(z, (oh_ref[...], ol_ref[...]))
    pred_ref[...] = pred
    target = t_ref[...]
    resid = pred - target
    err = jnp.sum(resid * resid, axis=0, keepdims=True)
    power = jnp.sum(target * target, axis=0, keepdims=True)
    sums = jnp.concatenate([err, power, jnp.zeros((6, err.shape[1]), F32)], axis=0)
    (zh, zl), (rh, rl) = z, split(resid)

    def dot_t(left, right):
        return lax.dot_general(left, right, (((0,), (0,)), ((), ())), preferred_element_type=F32)

    grad = dot_t(zh, rh) + (dot_t(zh, rl) + dot_t(zl, rh))
    half = width // 2
    swap = (me & 1) == 1
    top, bottom = grad[:half], grad[half:]
    keep_ref[:half] = jnp.where(swap, bottom, top)
    send_ref[:half] = jnp.where(swap, top, bottom)
    keep_ref[half:] = sums
    send_ref[half:] = sums


def flip(value, mask, count):
    return lax.ppermute(value, AXES, [(i, i ^ mask) for i in range(count)])


def pick(value, at):
    return lax.dynamic_index_in_dim(value, at, 0, keepdims=False)


def gather_all(payload, count):
    bits = count.bit_length() - 1
    groups = []
    top = bits
    while top > 1:
        low = max(1, top - 2)
        groups.append([m << low for m in range(1 << (top - low))])
        top = low
    masks = [0]
    table = payload[None]
    for group in groups:
        table = jnp.concatenate([table] + [flip(table, m, count) for m in group[1:]], axis=0)
        masks = [a ^ m for m in group for a in masks]
    return [table, flip(table, 1, count)], masks + [m ^ 1 for m in masks], groups


def gather_window(payload, reach):
    tiles = lax.all_gather(payload, "lon")
    n_lat = lax.axis_size("lat")
    bands = []
    for off in range(-reach, reach + 1):
        if off == 0:
            bands.append(tiles)
        else:
            pairs = [(i + off, i) for i in range(n_lat) if 0 <= i + off < n_lat]
            bands.append(lax.ppermute(tiles, "lat", pairs))
    return jnp.concatenate(bands, axis=0)


def shards(
    grid_in,
    target,
    w_enc,
    w_mix_self,
    w_mix_nbr,
    w_dec,
    w_out,
    var_weight,
    g2m_idx,
    g2m_w,
    mesh_nbr,
    m2g_idx,
    m2g_w,
):
    n_lat, n_lon = lax.axis_size("lat"), lax.axis_size("lon")
    count = n_lat * n_lon
    rows, width = grid_in.shape
    n_blocks = rows // BS
    nodes = g2m_idx.shape[0]
    k_g2m, k_nbr = g2m_idx.shape[1], mesh_nbr.shape[1]
    n_var = target.shape[1]
    band, tile = lax.axis_index("lat"), lax.axis_index("lon")
    me = band * n_lon + tile
    butterfly = count & (count - 1) == 0 and n_lat <= 9 and count >= 8
    reaches = (4, 3, 2, 1)
    if butterfly:
        widths = [min(2 * r + 1, n_lat) for r in reaches]
        starts = [jnp.clip(band - r, 0, n_lat - w) for r, w in zip(reaches, widths)]
        widths[0], starts[0] = n_lat, jnp.zeros_like(band)
    else:
        widths = [2 * r + 1 for r in reaches]
        starts = [band - r for r in reaches]
    scalars = jnp.stack([me] + starts).astype(jnp.int32)

    info = jnp.concatenate(
        [g2m_idx.astype(F32), g2m_w, mesh_nbr.astype(F32), jnp.zeros((nodes, GROUP - 2 * k_g2m - k_nbr), F32)], axis=1
    )
    info = info.reshape(nodes // 8, 8, GROUP).transpose(1, 0, 2).reshape(8, LANES)
    wide = (n_blocks // 8) * width + LANES
    h_one, payload = pl.pallas_call(
        encode_kernel,
        out_shape=(shape((rows, width)), shape((8, wide))),
        in_specs=[vmem()] * 3,
        out_specs=(vmem(), vmem()),
        compiler_params=pltpu.CompilerParams(vmem_limit_bytes=VMEM_LIMIT),
        name="encode",
    )(grid_in, w_enc, info)

    n2 = widths[3] * n_lon * nodes
    wh, wl, oh, ol, ah, al = pl.pallas_call(
        functools.partial(prepare_kernel, n_lon * nodes),
        out_shape=(
            shape((2 * L + 1, width, width), BF16),
            shape((2 * L + 1, width, width), BF16),
            shape((width, n_var), BF16),
            shape((width, n_var), BF16),
            shape((rows, n2), BF16),
            shape((rows, n2), BF16),
        ),
        in_specs=[smem()] + [vmem()] * 6,
        out_specs=[vmem()] * 6,
        compiler_params=pltpu.CompilerParams(vmem_limit_bytes=VMEM_LIMIT),
        cost_estimate=pl.CostEstimate(flops=0, bytes_accessed=12 * 1024 * 1024, transcendentals=0),
        name="prepare",
    )(scalars, w_mix_self, w_mix_nbr, w_dec, w_out, m2g_idx, m2g_w)

    if butterfly:
        tables, masks, groups = gather_all(payload, count)
    else:
        tables, masks = [gather_window(payload, reaches[0])], None
    plan = dict(tables=len(tables), xor=masks, lon=n_lon, blocks=n_blocks, nodes=nodes, k_g2m=k_g2m, k_nbr=k_nbr)
    nb = widths[0] * n_lon * n_blocks
    n0, n1 = (w * n_lon * nodes for w in widths[1:3])
    half = width // 2
    pred, keep, send = pl.pallas_call(
        functools.partial(mesh_kernel, plan),
        out_shape=(shape((rows, n_var)), shape((half + 8, n_var)), shape((half + 8, n_var))),
        in_specs=[smem()] + [vmem()] * (len(tables) + 8),
        out_specs=[vmem()] * 3,
        scratch_shapes=[
            pltpu.VMEM((nb, width), BF16),
            pltpu.VMEM((nb, width), BF16),
            pltpu.VMEM((widths[0] * n_lon, 8, LANES), F32),
            pltpu.VMEM((n0, width), F32),
            pltpu.VMEM((n0, width), BF16),
            pltpu.VMEM((n0, width), BF16),
            pltpu.VMEM((n1, width), F32),
            pltpu.VMEM((n1, width), BF16),
            pltpu.VMEM((n1, width), BF16),
            pltpu.VMEM((n2, width), BF16),
            pltpu.VMEM((n2, width), BF16),
        ],
        compiler_params=pltpu.CompilerParams(vmem_limit_bytes=VMEM_LIMIT),
        name="mesh",
    )(scalars, *tables, wh, wl, oh, ol, ah, al, h_one, target)

    weights = var_weight.astype(F32)
    wsum = jnp.sum(weights)
    grid_total = rows * count

    def factors(sums):
        scale = sums[1] / grid_total + 1e-06
        return sums[0], weights / (scale * grid_total * wsum)

    if not butterfly:
        swap = (me & 1) == 1
        top = jnp.where(swap, send[:half], keep[:half])
        bottom = jnp.where(swap, keep[:half], send[:half])
        total = lax.psum(jnp.concatenate([top, bottom, keep[half:]], axis=0), AXES)
        err, factor = factors(total[width:])
        return (pred, jnp.sum(err * factor), total[:width] * (2.0 * factor)[None, :])

    total = keep + flip(send, 1, count)
    group = groups[-1]
    low = len(group)
    at = (me >> 1) & (low - 1)
    part = half // low
    pieces, sums = total[:half].reshape(low, part, n_var), total[half:]
    total = jnp.concatenate([pick(pieces, at), sums], axis=0)
    for i, received in enumerate(
        [flip(jnp.concatenate([pick(pieces, at ^ i), sums], axis=0), m, count) for i, m in enumerate(group) if m]
    ):
        total = total + received
    for other in groups[-2::-1]:
        received = [flip(total, m, count) for m in other if m]
        for value in received:
            total = total + value
    err, factor = factors(total[part:])
    piece = total[:part] * (2.0 * factor)[None, :]
    pieces = jnp.stack([piece] + [flip(piece, m, count) for m in group if m])
    own = jnp.concatenate([pick(pieces, at ^ i) for i in range(low)], axis=0)
    other = flip(own, 1, count)
    swap = (me & 1) == 1
    grad_out = jnp.concatenate([jnp.where(swap, other, own), jnp.where(swap, own, other)], axis=0)
    return (pred, jnp.sum(err * factor), grad_out)


def solution(mesh):
    placed = (
        P(AXES, None),
        P(AXES, None),
        P(),
        P(),
        P(),
        P(),
        P(),
        P(),
        P(AXES, None),
        P(AXES, None),
        P(AXES, None),
        P(AXES, None),
        P(AXES, None),
    )
    return jax.shard_map(
        shards,
        mesh=mesh,
        in_specs=placed,
        out_specs=(P(AXES, None), P(), P()),
        check_vma=False,
    )
```

```python
import functools

import jax
import jax.numpy as jnp
from jax import lax
from jax.experimental import pallas as pl
from jax.experimental.pallas import tpu as pltpu
from jax.sharding import PartitionSpec as P

BS = 16
L = 2
REACHES = (4, 3, 2, 1)
AXES = ("lat", "lon")
F32 = jnp.float32
BF16 = jnp.bfloat16
LANES = 128
GROUP = 32
MIB = 1024 * 1024


def split(value):
    high = value.astype(BF16)
    return high, (value - high.astype(F32)).astype(BF16)


def dot(left, right):
    return jnp.dot(left, right, preferred_element_type=F32)


def dot3(left, right):
    (lh, ll), (rh, rl) = left, right
    return dot(lh, rh) + (dot(lh, rl) + dot(ll, rh))


def silu(value):
    return value / (1.0 + jnp.exp(-value))


def vmem():
    return pl.BlockSpec(memory_space=pltpu.VMEM)


def hbm():
    return pl.BlockSpec(memory_space=pltpu.MemorySpace.HBM)


def fetch(sources, places, sems):
    copies = [pltpu.make_async_copy(a, b, sems.at[i]) for i, (a, b) in enumerate(zip(sources, places))]
    for copy in copies:
        copy.start()
    return copies


def shape(dims, dtype=F32):
    return jax.ShapeDtypeStruct(dims, dtype)


def encode_kernel(x_hbm, w_hbm, info_ref, h_ref, p_ref, x_ref, w_ref, sems):
    copies = fetch((x_hbm, w_hbm), (x_ref, w_ref), sems)
    rows, width = x_ref.shape
    n_blocks = rows // BS
    p_ref[:, (n_blocks // 8) * width:] = info_ref[...]
    for copy in copies:
        copy.wait()
    x = x_ref[...]
    h = x + silu(dot3(split(x), split(w_ref[...])))
    h_ref[...] = h
    means = jnp.sum(h.reshape(n_blocks, BS, width), axis=1) * (1.0 / BS)
    for part in range(n_blocks // 8):
        p_ref[:, part * width:(part + 1) * width] = means[part * 8:(part + 1) * 8]


def band_starts(plan):
    band, tile = lax.axis_index("lat"), lax.axis_index("lon")
    starts = []
    for reach, bands in zip(REACHES, plan["bands"]):
        start = band - reach
        if plan["xor"] is not None:
            start = jnp.clip(start, 0, plan["lat"] - bands)
        starts.append(start)
    return band * plan["lon"] + tile, starts


def prepare_kernel(plan, ws_hbm, wn_hbm, wd_hbm, wo_hbm, near_ref, wh_ref, wl_ref, dh_ref, dl_ref, oh_ref, ol_ref, ah_ref, al_ref,
                   w_ref, wd_ref, wo_ref, params, sems):
    width = wd_hbm.shape[0]
    sources, places = [], []
    for layer in range(L):
        sources += [ws_hbm.at[layer], wn_hbm.at[layer]]
        places += [w_ref.at[2 * layer], w_ref.at[2 * layer + 1]]
    copies = fetch(sources + [wd_hbm, wo_hbm], places + [wd_ref, wo_ref], sems)
    rows, nodes = ah_ref.shape
    spread = near_ref.shape[0] // 2
    starts = band_starts(plan)[1]
    params[...] = jnp.zeros_like(params)
    params[:spread] = near_ref[:spread] - (starts[3] * (plan["lon"] * plan["nodes"])).astype(F32)
    params[spread:2 * spread] = near_ref[spread:] / jnp.sum(near_ref[spread:], axis=0, keepdims=True)
    turned = params[...].T
    local, coef = turned[:, :spread], turned[:, spread:2 * spread]
    step = 32
    column = lax.broadcasted_iota(jnp.int32, (step, nodes), 1).astype(F32)
    for at in range(0, rows, step):
        total = jnp.zeros((step, nodes), F32)
        for k in range(spread):
            total = total + jnp.where(column == local[at:at + step, k:k + 1], coef[at:at + step, k:k + 1], 0.0)
        ah_ref[at:at + step], al_ref[at:at + step] = split(total)
    for i in range(2 * L):
        copies[i].wait()
        at = slice((i % 2) * width, (i % 2 + 1) * width)
        wh_ref[i // 2, at], wl_ref[i // 2, at] = split(w_ref[i])
    copies[-2].wait()
    dh_ref[...], dl_ref[...] = split(wd_ref[...])
    copies[-1].wait()
    oh_ref[...], ol_ref[...] = split(wo_ref[...])


def mesh_kernel(plan, *refs):
    n_tables = plan["tables"]
    tables, refs = refs[:n_tables], refs[n_tables:]
    (wh_ref, wl_ref, dh_ref, dl_ref, oh_ref, ol_ref, ah_ref, al_ref, h_ref, t_ref, pred_ref, keep_ref, send_ref,
     th, tl, info, m0f, m0h, m0l, m1f, m1h, m1l, m2h, m2l, pred_buf, sem) = refs
    width = h_ref.shape[1]
    lon, n_blocks, nodes = plan["lon"], plan["blocks"], plan["nodes"]
    k_g2m, k_nbr = plan["k_g2m"], plan["k_nbr"]
    slots = tables[0].shape[0]
    me, (start_b, start0, start1, start2) = band_starts(plan)
    lane = lax.broadcasted_iota(jnp.int32, (8, LANES), 1)
    for c, table in enumerate(tables):
        for i in range(slots):
            if plan["xor"] is None:
                place = i
            else:
                place = me ^ plan["xor"][c * slots + i]
            tile = table[i]
            rows = jnp.concatenate([tile[:, p * width:(p + 1) * width] for p in range(n_blocks // 8)], axis=0)
            at = pl.multiple_of(place * n_blocks, n_blocks)
            th[pl.ds(at, n_blocks), :], tl[pl.ds(at, n_blocks), :] = split(rows)
            info[place] = tile[:, (n_blocks // 8) * width:]

    def band_rows(band, which):
        first = (band - start_b) * lon
        out = []
        for at in range(0, lon * nodes, LANES):
            total = None
            for d in range(LANES // nodes):
                tile = info[first + at // nodes + d]
                if d != which:
                    tile = pltpu.roll(tile, ((d - which) * nodes) % LANES, 1)
                if total is None:
                    total = tile
                else:
                    total = jnp.where(lane >= d * nodes, tile, total)
            out.append(total)
        return jnp.concatenate(out, axis=1)

    def near(band, start, bands, per_band):
        three = min(3, bands)
        low = jnp.clip(band - 1, start, start + bands - three)
        at = pl.multiple_of((low - start) * per_band, per_band)
        return pl.ds(at, three * per_band), (low * per_band).astype(F32)

    per_band, per_band_b = lon * nodes, lon * n_blocks
    row_b = lax.broadcasted_iota(jnp.int32, (min(3, plan["bands"][0]) * per_band_b, per_band), 0).astype(F32)
    for i in range(plan["bands"][1]):
        src, base = near(start0 + i, start_b, plan["bands"][0], per_band_b)
        local = band_rows(start0 + i, 0) - base
        coef = band_rows(start0 + i, 1)
        total = jnp.sum(coef, axis=0, keepdims=True)
        coef = coef / jnp.where(total == 0.0, 1.0, total)
        matrix = jnp.zeros(row_b.shape, F32)
        for k in range(k_g2m):
            matrix = matrix + jnp.where(row_b == local[k:k + 1], coef[k:k + 1], 0.0)
        matrix = matrix.T
        value = dot3(split(matrix), (th[src, :], tl[src, :]))
        at = slice(i * per_band, (i + 1) * per_band)
        m0f[at] = value
        m0h[at], m0l[at] = split(value)

    def mixing(layer, src, src_start, src_bands, out, out_start, out_bands):
        srcf, srch, srcl = src
        row = lax.broadcasted_iota(jnp.int32, (min(3, src_bands) * per_band, per_band), 0).astype(F32)
        for i in range(out_bands):
            band = out_start + i
            rows, base = near(band, src_start, src_bands, per_band)

            local = band_rows(band, 2) - base
            matrix = jnp.zeros(row.shape, F32)
            for k in range(k_nbr):
                matrix = matrix + jnp.where(row == local[k:k + 1], 1.0, 0.0)
            matrix = matrix.T.astype(BF16)
            agg = (dot(matrix, srch[rows, :]) + dot(matrix, srcl[rows, :])) * (1.0 / k_nbr)
            own = srcf[pl.ds(pl.multiple_of((band - src_start) * per_band, per_band), per_band), :]
            center = own - jnp.mean(own, axis=1, keepdims=True)
            nrm = center * (1.0 / jnp.sqrt(jnp.mean(center * center, axis=1, keepdims=True) + 1e-05))
            value = own + silu(dot3(split(jnp.concatenate([nrm, agg], axis=1)), (wh_ref[layer], wl_ref[layer])))
            at = slice(i * per_band, (i + 1) * per_band)
            if out[0] is not None:
                out[0][at] = value
            out[1][at], out[2][at] = split(value)

    _, bands0, bands1, bands2 = plan["bands"]
    mixing(0, (m0f, m0h, m0l), start0, bands0, (m1f, m1h, m1l), start1, bands1)
    mixing(1, (m1f, m1h, m1l), start1, bands1, (None, m2h, m2l), start2, bands2)

    x = h_ref[...] + dot3((ah_ref[...], al_ref[...]), (m2h[...], m2l[...]))
    z = split(silu(dot3(split(x), (dh_ref[...], dl_ref[...]))))
    pred = dot3(z, (oh_ref[...], ol_ref[...]))
    pred_buf[...] = pred
    out = pltpu.make_async_copy(pred_buf, pred_ref, sem)
    out.start()
    target = t_ref[...]
    resid = pred - target
    err = jnp.sum(resid * resid, axis=0, keepdims=True)
    power = jnp.sum(target * target, axis=0, keepdims=True)
    sums = jnp.concatenate([err, power, jnp.zeros((6, err.shape[1]), F32)], axis=0)
    (zh, zl), (rh, rl) = z, split(resid)

    def dot_t(left, right):
        return lax.dot_general(left, right, (((0,), (0,)), ((), ())), preferred_element_type=F32)

    grad = dot_t(zh, rh) + (dot_t(zh, rl) + dot_t(zl, rh))
    half = width // 2
    swap = (me & 1) == 1
    top, bottom = grad[:half], grad[half:]
    keep_ref[:half] = jnp.where(swap, bottom, top)
    send_ref[:half] = jnp.where(swap, top, bottom)
    keep_ref[half:] = sums
    send_ref[half:] = sums
    out.wait()


def flip(value, mask, count):
    return lax.ppermute(value, AXES, [(i, i ^ mask) for i in range(count)])


def pick(value, at):
    return lax.dynamic_index_in_dim(value, at, 0, keepdims=False)


def gather_all(payload, groups, count, beside):
    table = payload[None]
    for group in groups:
        parts = [table] + [flip(table, m, count) for m in group[1:]]
        if group is groups[-1]:
            parts, beside = lax.optimization_barrier((parts, beside))
        table = jnp.concatenate(parts, axis=0)
    return [table, flip(table, 1, count)], beside


def gather_window(payload, reach):
    tiles = lax.all_gather(payload, "lon")
    n_lat = lax.axis_size("lat")
    bands = []
    for off in range(-reach, reach + 1):
        if off == 0:
            bands.append(tiles)
        else:
            pairs = [(i + off, i) for i in range(n_lat) if 0 <= i + off < n_lat]
            bands.append(lax.ppermute(tiles, "lat", pairs))
    return jnp.concatenate(bands, axis=0)


def shards(
    grid_in,
    target,
    w_enc,
    w_mix_self,
    w_mix_nbr,
    w_dec,
    w_out,
    var_weight,
    g2m_idx,
    g2m_w,
    mesh_nbr,
    m2g_idx,
    m2g_w,
):
    n_lat, n_lon = lax.axis_size("lat"), lax.axis_size("lon")
    count = n_lat * n_lon
    rows, width = grid_in.shape
    n_blocks = rows // BS
    nodes = g2m_idx.shape[0]
    k_g2m, k_nbr = g2m_idx.shape[1], mesh_nbr.shape[1]
    n_var = target.shape[1]
    band, tile = lax.axis_index("lat"), lax.axis_index("lon")
    me = band * n_lon + tile
    butterfly = count & (count - 1) == 0 and n_lat <= 9 and count >= 8
    if butterfly:
        bands = [n_lat] + [min(2 * r + 1, n_lat) for r in REACHES[1:]]
        bits = count.bit_length() - 1
        groups = []
        while bits > 1:
            low = max(1, bits - 2)
            groups.append([m << low for m in range(1 << (bits - low))])
            bits = low
        masks = [0]
        for group in groups:
            masks = [a ^ m for m in group for a in masks]
        masks = masks + [m ^ 1 for m in masks]
    else:
        bands = [2 * r + 1 for r in REACHES]
        masks = None
    plan = dict(
        tables=2 if butterfly else 1, xor=masks, bands=bands, lat=n_lat, lon=n_lon,
        blocks=n_blocks, nodes=nodes, k_g2m=k_g2m, k_nbr=k_nbr,
    )
    def place(value, at):
        return jnp.pad(value.T, ((0, 8 - value.shape[1]), (at * nodes, LANES - (at + 1) * nodes)))

    info = (place(g2m_idx, 0) + place(mesh_nbr, 2)).astype(F32) + place(g2m_w, 1)
    wide = (n_blocks // 8) * width + LANES
    h_one, payload = pl.pallas_call(
        encode_kernel,
        out_shape=(shape((rows, width)), shape((8, wide))),
        in_specs=[hbm(), hbm(), vmem()],
        out_specs=(vmem(), vmem()),
        scratch_shapes=[
            pltpu.VMEM(grid_in.shape, F32),
            pltpu.VMEM(w_enc.shape, F32),
            pltpu.SemaphoreType.DMA((2,)),
        ],
        compiler_params=pltpu.CompilerParams(vmem_limit_bytes=53 * MIB),
        name="encode",
    )(grid_in, w_enc, info)

    k_m2g = m2g_idx.shape[1]
    near = jnp.pad(m2g_idx.T, ((0, k_m2g), (0, 0))).astype(F32) + jnp.pad(m2g_w.T, ((k_m2g, 0), (0, 0)))
    n2 = bands[3] * n_lon * nodes
    prepared = pl.pallas_call(
        functools.partial(prepare_kernel, plan),
        out_shape=(
            shape((L, 2 * width, width), BF16),
            shape((L, 2 * width, width), BF16),
            shape((width, width), BF16),
            shape((width, width), BF16),
            shape((width, n_var), BF16),
            shape((width, n_var), BF16),
            shape((rows, n2), BF16),
            shape((rows, n2), BF16),
        ),
        in_specs=[hbm()] * 4 + [vmem()],
        out_specs=[vmem()] * 8,
        scratch_shapes=[
            pltpu.VMEM((2 * L, width, width), F32),
            pltpu.VMEM(w_dec.shape, F32),
            pltpu.VMEM(w_out.shape, F32),
            pltpu.VMEM((LANES, rows), F32),
            pltpu.SemaphoreType.DMA((2 * L + 2,)),
        ],
        compiler_params=pltpu.CompilerParams(vmem_limit_bytes=47 * MIB),
        cost_estimate=pl.CostEstimate(flops=0, bytes_accessed=12 * 1024 * 1024, transcendentals=0),
        name="prepare",
    )(w_mix_self, w_mix_nbr, w_dec, w_out, near)

    if butterfly:
        tables, prepared = gather_all(payload, groups, count, prepared)
    else:
        tables = [gather_window(payload, REACHES[0])]
    nb = bands[0] * n_lon * n_blocks
    n0, n1 = (w * n_lon * nodes for w in bands[1:3])
    half = width // 2
    pred, keep, send = pl.pallas_call(
        functools.partial(mesh_kernel, plan),
        out_shape=(shape((rows, n_var)), shape((half + 8, n_var)), shape((half + 8, n_var))),
        in_specs=[vmem()] * (len(tables) + 10),
        out_specs=[hbm(), vmem(), vmem()],
        scratch_shapes=[
            pltpu.VMEM((nb, width), BF16),
            pltpu.VMEM((nb, width), BF16),
            pltpu.VMEM((bands[0] * n_lon, 8, LANES), F32),
            pltpu.VMEM((n0, width), F32),
            pltpu.VMEM((n0, width), BF16),
            pltpu.VMEM((n0, width), BF16),
            pltpu.VMEM((n1, width), F32),
            pltpu.VMEM((n1, width), BF16),
            pltpu.VMEM((n1, width), BF16),
            pltpu.VMEM((n2, width), BF16),
            pltpu.VMEM((n2, width), BF16),
            pltpu.VMEM((rows, n_var), F32),
            pltpu.SemaphoreType.DMA(()),
        ],
        compiler_params=pltpu.CompilerParams(vmem_limit_bytes=32 * MIB),
        name="mesh",
    )(*tables, *prepared, h_one, target)

    weights = var_weight.astype(F32)
    wsum = jnp.sum(weights)
    grid_total = rows * count

    def factors(sums):
        scale = sums[1] / grid_total + 1e-06
        return sums[0], weights / (scale * grid_total * wsum)

    if not butterfly:
        swap = (me & 1) == 1
        top = jnp.where(swap, send[:half], keep[:half])
        bottom = jnp.where(swap, keep[:half], send[:half])
        total = lax.psum(jnp.concatenate([top, bottom, keep[half:]], axis=0), AXES)
        err, factor = factors(total[width:])
        return (pred, jnp.sum(err * factor), total[:width] * (2.0 * factor)[None, :])

    total = keep + flip(send, 1, count)
    group = groups[-1]
    low = len(group)
    at = (me >> 1) & (low - 1)
    part = half // low
    pieces, sums = total[:half].reshape(low, part, n_var), total[half:]
    total = jnp.concatenate([pick(pieces, at), sums], axis=0)
    for i, received in enumerate(
        [flip(jnp.concatenate([pick(pieces, at ^ i), sums], axis=0), m, count) for i, m in enumerate(group) if m]
    ):
        total = total + received
    for other in groups[-2::-1]:
        received = [flip(total, m, count) for m in other if m]
        for value in received:
            total = total + value
    err, factor = factors(total[part:])
    piece = total[:part] * (2.0 * factor)[None, :]
    pieces = jnp.stack([piece] + [flip(piece, m, count) for m in group if m])
    own = jnp.concatenate([pick(pieces, at ^ i) for i in range(low)], axis=0)
    other = flip(own, 1, count)
    swap = (me & 1) == 1
    grad_out = jnp.concatenate([jnp.where(swap, other, own), jnp.where(swap, own, other)], axis=0)
    return (pred, jnp.sum(err * factor), grad_out)


def solution(mesh):
    placed = (
        P(AXES, None),
        P(AXES, None),
        P(),
        P(),
        P(),
        P(),
        P(),
        P(),
        P(AXES, None),
        P(AXES, None),
        P(AXES, None),
        P(AXES, None),
        P(AXES, None),
    )
    return jax.shard_map(
        shards,
        mesh=mesh,
        in_specs=placed,
        out_specs=(P(AXES, None), P(), P()),
        check_vma=False,
    )
```

```python
import functools

import jax
import jax.numpy as jnp
from jax import lax
from jax.experimental import pallas as pl
from jax.experimental.pallas import tpu as pltpu
from jax.sharding import PartitionSpec as P

BS = 16
L = 2
REACHES = (4, 3, 2, 1)
AXES = ("lat", "lon")
F32 = jnp.float32
BF16 = jnp.bfloat16
LANES = 128
GROUP = 32
MIB = 1024 * 1024
AHEAD = 1
DENSE = (1, 1)
CHUNKS = 2


def split(value):
    high = value.astype(BF16)
    return high, (value - high.astype(F32)).astype(BF16)


def dot(left, right):
    return jnp.dot(left, right, preferred_element_type=F32)


def dot3(left, right):
    (lh, ll), (rh, rl) = left, right
    return dot(lh, rh) + (dot(lh, rl) + dot(ll, rh))


def silu(value):
    return value / (1.0 + jnp.exp(-value))


def vmem():
    return pl.BlockSpec(memory_space=pltpu.VMEM)


def hbm():
    return pl.BlockSpec(memory_space=pltpu.MemorySpace.HBM)


def fetch(sources, places, sems):
    copies = [pltpu.make_async_copy(a, b, sems.at[i]) for i, (a, b) in enumerate(zip(sources, places))]
    for copy in copies:
        copy.start()
    return copies


def shape(dims, dtype=F32):
    return jax.ShapeDtypeStruct(dims, dtype)


def encode_kernel(x_hbm, w_hbm, h_ref, p_ref, x_ref, w_ref, sems):
    rows, width = x_ref.shape
    n_blocks = rows // BS
    part = width // CHUNKS
    sources = [x_hbm] + [w_hbm.at[pl.ds(i * part, part), :] for i in range(CHUNKS)]
    places = [x_ref] + [w_ref.at[pl.ds(i * part, part), :] for i in range(CHUNKS)]
    copies = fetch(sources, places, sems)
    copies[0].wait()
    x = x_ref[...]
    high, low = split(x)
    total = jnp.zeros(x.shape, F32)
    for i in range(CHUNKS):
        copies[1 + i].wait()
        at = slice(i * part, (i + 1) * part)
        total = total + dot3((high[:, at], low[:, at]), split(w_ref[at]))
    h = x + silu(total)
    h_ref[...] = h
    means = jnp.sum(h.reshape(n_blocks, BS, width), axis=1) * (1.0 / BS)
    for i in range(n_blocks // 8):
        p_ref[:, i * width:(i + 1) * width] = means[i * 8:(i + 1) * 8]


def pack_kernel(m_ref, gi_ref, gw_ref, ni_ref, p_ref, params):
    spread, nodes = gi_ref.shape
    params[...] = jnp.zeros_like(params)
    params[:spread, :nodes] = gi_ref[...].astype(F32)
    params[8:8 + spread, :nodes] = gw_ref[...]
    params[16:16 + ni_ref.shape[0], :nodes] = ni_ref[...].astype(F32)
    tile = params[:8]
    for i in (1, 2):
        tile = tile + pltpu.roll(params[8 * i:8 * i + 8], i * nodes, 1)
    wide = m_ref.shape[1]
    p_ref[:, :wide] = m_ref[...]
    p_ref[:, wide:] = tile


def band_starts(plan):
    band, tile = lax.axis_index("lat"), lax.axis_index("lon")
    starts = []
    for reach, bands in zip(REACHES, plan["bands"]):
        start = band - reach
        if plan["xor"] is not None:
            start = jnp.clip(start, 0, plan["lat"] - bands)
        starts.append(start)
    return band * plan["lon"] + tile, starts


def prepare_kernel(plan, ws_hbm, wn_hbm, wd_hbm, wo_hbm, near_ref, wh_ref, wl_ref, dh_ref, dl_ref, oh_ref, ol_ref, ah_ref, al_ref,
                   w_ref, wd_ref, wo_ref, params, sems):
    width = wd_hbm.shape[0]
    sources, places = [], []
    for layer in range(L):
        sources += [ws_hbm.at[layer], wn_hbm.at[layer]]
        places += [w_ref.at[2 * layer], w_ref.at[2 * layer + 1]]
    copies = fetch(sources + [wd_hbm, wo_hbm], places + [wd_ref, wo_ref], sems)
    rows, nodes = ah_ref.shape
    spread = near_ref.shape[0] // 2
    starts = band_starts(plan)[1]
    params[...] = jnp.zeros_like(params)
    params[:spread] = near_ref[:spread] - (starts[3] * (plan["lon"] * plan["nodes"])).astype(F32)
    params[spread:2 * spread] = near_ref[spread:] / jnp.sum(near_ref[spread:], axis=0, keepdims=True)
    turned = params[...].T
    local, coef = turned[:, :spread], turned[:, spread:2 * spread]
    step = 32
    column = lax.broadcasted_iota(jnp.int32, (step, nodes), 1).astype(F32)
    for at in range(0, rows, step):
        total = jnp.zeros((step, nodes), F32)
        for k in range(spread):
            total = total + jnp.where(column == local[at:at + step, k:k + 1], coef[at:at + step, k:k + 1], 0.0)
        ah_ref[at:at + step], al_ref[at:at + step] = split(total)
    for i in range(2 * L):
        copies[i].wait()
        at = slice((i % 2) * width, (i % 2 + 1) * width)
        wh_ref[i // 2, at], wl_ref[i // 2, at] = split(w_ref[i])
    copies[-2].wait()
    dh_ref[...], dl_ref[...] = split(wd_ref[...])
    copies[-1].wait()
    oh_ref[...], ol_ref[...] = split(wo_ref[...])


def mesh_kernel(plan, *refs):
    n_tables = plan["tables"]
    tables, refs = refs[:n_tables], refs[n_tables:]
    (wh_ref, wl_ref, dh_ref, dl_ref, oh_ref, ol_ref, ah_ref, al_ref, h_ref, t_ref, pred_ref, keep_ref, send_ref,
     th, tl, info, m0f, m0h, m0l, m1f, m1h, m1l, m2h, m2l, xh, xl, pred_buf, sem) = refs
    width = h_ref.shape[1]
    lon, n_blocks, nodes = plan["lon"], plan["blocks"], plan["nodes"]
    k_g2m, k_nbr = plan["k_g2m"], plan["k_nbr"]
    slots = tables[0].shape[0]
    me, (start_b, start0, start1, start2) = band_starts(plan)
    lane = lax.broadcasted_iota(jnp.int32, (8, LANES), 1)
    for c, table in enumerate(tables):
        for i in range(slots):
            if plan["xor"] is None:
                place = i
            else:
                place = me ^ plan["xor"][c * slots + i]
            tile = table[i]
            rows = jnp.concatenate([tile[:, p * width:(p + 1) * width] for p in range(n_blocks // 8)], axis=0)
            at = pl.multiple_of(place * n_blocks, n_blocks)
            th[pl.ds(at, n_blocks), :], tl[pl.ds(at, n_blocks), :] = split(rows)
            info[place] = tile[:, (n_blocks // 8) * width:]

    def band_rows(band, which):
        first = (band - start_b) * lon
        out = []
        for at in range(0, lon * nodes, LANES):
            total = None
            for d in range(LANES // nodes):
                tile = info[first + at // nodes + d]
                if d != which:
                    tile = pltpu.roll(tile, ((d - which) * nodes) % LANES, 1)
                if total is None:
                    total = tile
                else:
                    total = jnp.where(lane >= d * nodes, tile, total)
            out.append(total)
        return jnp.concatenate(out, axis=1)

    def near(band, start, bands, per_band):
        three = min(3, bands)
        low = jnp.clip(band - 1, start, start + bands - three)
        at = pl.multiple_of((low - start) * per_band, per_band)
        return pl.ds(at, three * per_band), (low * per_band).astype(F32)

    per_band, per_band_b = lon * nodes, lon * n_blocks
    steps = []

    def to_mesh(i):
        src, base = near(start0 + i, start_b, plan["bands"][0], per_band_b)

        def build():
            row = lax.broadcasted_iota(jnp.int32, (min(3, plan["bands"][0]) * per_band_b, per_band), 0).astype(F32)
            local = band_rows(start0 + i, 0) - base
            coef = band_rows(start0 + i, 1)
            total = jnp.sum(coef, axis=0, keepdims=True)
            coef = coef / jnp.where(total == 0.0, 1.0, total)
            matrix = jnp.zeros(row.shape, F32)
            for k in range(k_g2m):
                matrix = matrix + jnp.where(row == local[k:k + 1], coef[k:k + 1], 0.0)
            return split(matrix.T)

        def run(matrix):
            value = dot3(matrix, (th[src, :], tl[src, :]))
            at = slice(i * per_band, (i + 1) * per_band)
            m0f[at] = value
            m0h[at], m0l[at] = split(value)

        return build, run

    def mixing(layer, i, src, src_start, src_bands, out, out_start):
        srcf, srch, srcl = src
        band = out_start + i
        rows, base = near(band, src_start, src_bands, per_band)

        def build():
            row = lax.broadcasted_iota(jnp.int32, (LANES, per_band), 0).astype(F32).astype(BF16)
            one, none = jnp.ones((), BF16), jnp.zeros((), BF16)
            local = band_rows(band, 2) - base
            pieces = []
            for at in range(0, min(3, src_bands) * per_band, LANES):
                piece = jnp.zeros(row.shape, BF16)
                here = (local - float(at)).astype(BF16)
                for k in range(k_nbr):
                    piece = piece + jnp.where(row == here[k:k + 1], one, none)
                pieces.append(piece.T)
            return jnp.concatenate(pieces, axis=1)

        def run(matrix):
            agg = (dot(matrix, srch[rows, :]) + dot(matrix, srcl[rows, :])) * (1.0 / k_nbr)
            own = srcf[pl.ds(pl.multiple_of((band - src_start) * per_band, per_band), per_band), :]
            center = own - jnp.mean(own, axis=1, keepdims=True)
            nrm = center * (1.0 / jnp.sqrt(jnp.mean(center * center, axis=1, keepdims=True) + 1e-05))
            at = slice(i * per_band, (i + 1) * per_band)
            xh[at, :width], xl[at, :width] = split(nrm)
            xh[at, width:], xl[at, width:] = split(agg)

        return build, run

    def dense(layer, srcf, shift, rows, out):
        def run(_):
            for at in range(0, rows, DENSE[layer] * per_band):
                part = min(DENSE[layer] * per_band, rows - at)
                here = slice(at, at + part)
                own = srcf[pl.ds(pl.multiple_of(shift * per_band + at, per_band), part), :]
                value = own + silu(dot3((xh[here], xl[here]), (wh_ref[layer], wl_ref[layer])))
                if out[0] is not None:
                    out[0][here] = value
                out[1][here], out[2][here] = split(value)

        return (lambda: None), run

    _, bands0, bands1, bands2 = plan["bands"]
    steps += [to_mesh(i) for i in range(bands0)]
    steps += [mixing(0, i, (m0f, m0h, m0l), start0, bands0, (m1f, m1h, m1l), start1) for i in range(bands1)]
    steps += [dense(0, m0f, start1 - start0, bands1 * per_band, (m1f, m1h, m1l))]
    steps += [mixing(1, i, (m1f, m1h, m1l), start1, bands1, (None, m2h, m2l), start2) for i in range(bands2)]
    steps += [dense(1, m1f, start2 - start1, bands2 * per_band, (None, m2h, m2l))]
    ready = [build() for build, _ in steps[:AHEAD]]
    for i, (_, run) in enumerate(steps):
        if i + AHEAD < len(steps):
            ready.append(steps[i + AHEAD][0]())
        run(ready.pop(0))

    x = h_ref[...] + dot3((ah_ref[...], al_ref[...]), (m2h[...], m2l[...]))
    z = split(silu(dot3(split(x), (dh_ref[...], dl_ref[...]))))
    pred = dot3(z, (oh_ref[...], ol_ref[...]))
    pred_buf[...] = pred
    out = pltpu.make_async_copy(pred_buf, pred_ref, sem)
    out.start()
    target = t_ref[...]
    resid = pred - target
    err = jnp.sum(resid * resid, axis=0, keepdims=True)
    power = jnp.sum(target * target, axis=0, keepdims=True)
    sums = jnp.concatenate([err, power, jnp.zeros((6, err.shape[1]), F32)], axis=0)
    (zh, zl), (rh, rl) = z, split(resid)

    def dot_t(left, right):
        return lax.dot_general(left, right, (((0,), (0,)), ((), ())), preferred_element_type=F32)

    grad = dot_t(zh, rh) + (dot_t(zh, rl) + dot_t(zl, rh))
    half = width // 2
    swap = (me & 1) == 1
    top, bottom = grad[:half], grad[half:]
    keep_ref[:half] = jnp.where(swap, bottom, top)
    send_ref[:half] = jnp.where(swap, top, bottom)
    keep_ref[half:] = sums
    send_ref[half:] = sums
    out.wait()


def flip(value, mask, count):
    return lax.ppermute(value, AXES, [(i, i ^ mask) for i in range(count)])


def pick(value, at):
    return lax.dynamic_index_in_dim(value, at, 0, keepdims=False)


def gather_all(payload, groups, count, beside):
    table = payload[None]
    for group in groups:
        parts = [table] + [flip(table, m, count) for m in group[1:]]
        if group is groups[-1]:
            parts, beside = lax.optimization_barrier((parts, beside))
        table = jnp.concatenate(parts, axis=0)
    return [table, flip(table, 1, count)], beside


def gather_window(payload, reach):
    tiles = lax.all_gather(payload, "lon")
    n_lat = lax.axis_size("lat")
    bands = []
    for off in range(-reach, reach + 1):
        if off == 0:
            bands.append(tiles)
        else:
            pairs = [(i + off, i) for i in range(n_lat) if 0 <= i + off < n_lat]
            bands.append(lax.ppermute(tiles, "lat", pairs))
    return jnp.concatenate(bands, axis=0)


def shards(
    grid_in,
    target,
    w_enc,
    w_mix_self,
    w_mix_nbr,
    w_dec,
    w_out,
    var_weight,
    g2m_idx,
    g2m_w,
    mesh_nbr,
    m2g_idx,
    m2g_w,
):
    n_lat, n_lon = lax.axis_size("lat"), lax.axis_size("lon")
    count = n_lat * n_lon
    rows, width = grid_in.shape
    n_blocks = rows // BS
    nodes = g2m_idx.shape[0]
    k_g2m, k_nbr = g2m_idx.shape[1], mesh_nbr.shape[1]
    n_var = target.shape[1]
    band, tile = lax.axis_index("lat"), lax.axis_index("lon")
    me = band * n_lon + tile
    butterfly = count & (count - 1) == 0 and n_lat <= 9 and count >= 8
    if butterfly:
        bands = [n_lat] + [min(2 * r + 1, n_lat) for r in REACHES[1:]]
        bits = count.bit_length() - 1
        groups = []
        while bits > 1:
            low = max(1, bits - 2)
            groups.append([m << low for m in range(1 << (bits - low))])
            bits = low
        masks = [0]
        for group in groups:
            masks = [a ^ m for m in group for a in masks]
        masks = masks + [m ^ 1 for m in masks]
    else:
        bands = [2 * r + 1 for r in REACHES]
        masks = None
    plan = dict(
        tables=2 if butterfly else 1, xor=masks, bands=bands, lat=n_lat, lon=n_lon,
        blocks=n_blocks, nodes=nodes, k_g2m=k_g2m, k_nbr=k_nbr,
    )
    wide = (n_blocks // 8) * width
    h_one, means = pl.pallas_call(
        encode_kernel,
        out_shape=(shape((rows, width)), shape((8, wide))),
        in_specs=[hbm()] * 2,
        out_specs=(vmem(), vmem()),
        scratch_shapes=[
            pltpu.VMEM(grid_in.shape, F32),
            pltpu.VMEM(w_enc.shape, F32),
            pltpu.SemaphoreType.DMA((1 + CHUNKS,)),
        ],
        compiler_params=pltpu.CompilerParams(vmem_limit_bytes=53 * MIB),
        name="encode",
        cost_estimate=pl.CostEstimate(flops=4 * 10**9, bytes_accessed=2 * MIB, transcendentals=0),
    )(grid_in, w_enc)
    payload = pl.pallas_call(
        pack_kernel,
        out_shape=shape((8, wide + LANES)),
        in_specs=[vmem()] * 4,
        out_specs=vmem(),
        scratch_shapes=[pltpu.VMEM((24, LANES), F32)],
        compiler_params=pltpu.CompilerParams(vmem_limit_bytes=4 * MIB),
        name="pack",
    )(means, g2m_idx.T, g2m_w.T, mesh_nbr.T)

    k_m2g = m2g_idx.shape[1]
    near = jnp.pad(m2g_idx.T, ((0, k_m2g), (0, 0))).astype(F32) + jnp.pad(m2g_w.T, ((k_m2g, 0), (0, 0)))
    n2 = bands[3] * n_lon * nodes
    prepared = pl.pallas_call(
        functools.partial(prepare_kernel, plan),
        out_shape=(
            shape((L, 2 * width, width), BF16),
            shape((L, 2 * width, width), BF16),
            shape((width, width), BF16),
            shape((width, width), BF16),
            shape((width, n_var), BF16),
            shape((width, n_var), BF16),
            shape((rows, n2), BF16),
            shape((rows, n2), BF16),
        ),
        in_specs=[hbm()] * 4 + [vmem()],
        out_specs=[vmem()] * 8,
        scratch_shapes=[
            pltpu.VMEM((2 * L, width, width), F32),
            pltpu.VMEM(w_dec.shape, F32),
            pltpu.VMEM(w_out.shape, F32),
            pltpu.VMEM((LANES, rows), F32),
            pltpu.SemaphoreType.DMA((2 * L + 2,)),
        ],
        compiler_params=pltpu.CompilerParams(vmem_limit_bytes=47 * MIB),
        cost_estimate=pl.CostEstimate(flops=0, bytes_accessed=12 * 1024 * 1024, transcendentals=0),
        name="prepare",
    )(w_mix_self, w_mix_nbr, w_dec, w_out, near)

    if butterfly:
        tables, prepared = gather_all(payload, groups, count, prepared)
    else:
        tables = [gather_window(payload, REACHES[0])]
    nb = bands[0] * n_lon * n_blocks
    n0, n1 = (w * n_lon * nodes for w in bands[1:3])
    half = width // 2
    pred, keep, send = pl.pallas_call(
        functools.partial(mesh_kernel, plan),
        out_shape=(shape((rows, n_var)), shape((half + 8, n_var)), shape((half + 8, n_var))),
        in_specs=[vmem()] * (len(tables) + 10),
        out_specs=[hbm(), vmem(), vmem()],
        scratch_shapes=[
            pltpu.VMEM((nb, width), BF16),
            pltpu.VMEM((nb, width), BF16),
            pltpu.VMEM((bands[0] * n_lon, 8, LANES), F32),
            pltpu.VMEM((n0, width), F32),
            pltpu.VMEM((n0, width), BF16),
            pltpu.VMEM((n0, width), BF16),
            pltpu.VMEM((n1, width), F32),
            pltpu.VMEM((n1, width), BF16),
            pltpu.VMEM((n1, width), BF16),
            pltpu.VMEM((n2, width), BF16),
            pltpu.VMEM((n2, width), BF16),
            pltpu.VMEM((n1, 2 * width), BF16),
            pltpu.VMEM((n1, 2 * width), BF16),
            pltpu.VMEM((rows, n_var), F32),
            pltpu.SemaphoreType.DMA(()),
        ],
        compiler_params=pltpu.CompilerParams(vmem_limit_bytes=32 * MIB),
        name="mesh",
    )(*tables, *prepared, h_one, target)

    weights = var_weight.astype(F32)
    wsum = jnp.sum(weights)
    grid_total = rows * count

    def factors(sums):
        scale = sums[1] / grid_total + 1e-06
        return sums[0], weights / (scale * grid_total * wsum)

    if not butterfly:
        swap = (me & 1) == 1
        top = jnp.where(swap, send[:half], keep[:half])
        bottom = jnp.where(swap, keep[:half], send[:half])
        total = lax.psum(jnp.concatenate([top, bottom, keep[half:]], axis=0), AXES)
        err, factor = factors(total[width:])
        return (pred, jnp.sum(err * factor), total[:width] * (2.0 * factor)[None, :])

    total = keep + flip(send, 1, count)
    group = groups[-1]
    low = len(group)
    at = (me >> 1) & (low - 1)
    part = half // low
    pieces, sums = total[:half].reshape(low, part, n_var), total[half:]
    total = jnp.concatenate([pick(pieces, at), sums], axis=0)
    for i, received in enumerate(
        [flip(jnp.concatenate([pick(pieces, at ^ i), sums], axis=0), m, count) for i, m in enumerate(group) if m]
    ):
        total = total + received
    for other in groups[-2::-1]:
        received = [flip(total, m, count) for m in other if m]
        for value in received:
            total = total + value
    err, factor = factors(total[part:])
    piece = total[:part] * (2.0 * factor)[None, :]
    pieces = jnp.stack([piece] + [flip(piece, m, count) for m in group if m])
    own = jnp.concatenate([pick(pieces, at ^ i) for i in range(low)], axis=0)
    other = flip(own, 1, count)
    swap = (me & 1) == 1
    grad_out = jnp.concatenate([jnp.where(swap, other, own), jnp.where(swap, own, other)], axis=0)
    return (pred, jnp.sum(err * factor), grad_out)


def solution(mesh):
    placed = (
        P(AXES, None),
        P(AXES, None),
        P(),
        P(),
        P(),
        P(),
        P(),
        P(),
        P(AXES, None),
        P(AXES, None),
        P(AXES, None),
        P(AXES, None),
        P(AXES, None),
    )
    return jax.shard_map(
        shards,
        mesh=mesh,
        in_specs=placed,
        out_specs=(P(AXES, None), P(), P()),
        check_vma=False,
    )
```

```python
import functools

import jax
import jax.numpy as jnp
from jax import lax
from jax.experimental import pallas as pl
from jax.experimental.pallas import tpu as pltpu
from jax.sharding import PartitionSpec as P

BS = 16
L = 2
REACHES = (4, 3, 2, 1)
AXES = ("lat", "lon")
F32 = jnp.float32
BF16 = jnp.bfloat16
LANES = 128
GROUP = 32
MIB = 1024 * 1024
CHUNKS = 2


def split(value):
    high = value.astype(BF16)
    return high, (value - high.astype(F32)).astype(BF16)


def dot(left, right):
    return jnp.dot(left, right, preferred_element_type=F32)


def dot3(left, right):
    (lh, ll), (rh, rl) = left, right
    return dot(lh, rh) + (dot(lh, rl) + dot(ll, rh))


def silu(value):
    return value / (1.0 + jnp.exp(-value))


def second_half(number, bits):
    half = number >> bits[0]
    for bit in bits[1:]:
        half = half ^ (number >> bit)
    return (half & 1) == 1


def vmem():
    return pl.BlockSpec(memory_space=pltpu.VMEM)


def hbm():
    return pl.BlockSpec(memory_space=pltpu.MemorySpace.HBM)


def fetch(sources, places, sems):
    copies = [pltpu.make_async_copy(a, b, sems.at[i]) for i, (a, b) in enumerate(zip(sources, places))]
    for copy in copies:
        copy.start()
    return copies


def shape(dims, dtype=F32):
    return jax.ShapeDtypeStruct(dims, dtype)


def encode_kernel(x_hbm, w_hbm, h_ref, p_ref, x_ref, w_ref, sems):
    rows, width = x_ref.shape
    n_blocks = rows // BS
    part = width // CHUNKS
    sources = [x_hbm] + [w_hbm.at[pl.ds(i * part, part), :] for i in range(CHUNKS)]
    places = [x_ref] + [w_ref.at[pl.ds(i * part, part), :] for i in range(CHUNKS)]
    copies = fetch(sources, places, sems)
    copies[0].wait()
    x = x_ref[...]
    high, low = split(x)
    total = jnp.zeros(x.shape, F32)
    for i in range(CHUNKS):
        copies[1 + i].wait()
        at = slice(i * part, (i + 1) * part)
        total = total + dot3((high[:, at], low[:, at]), split(w_ref[at]))
    h = x + silu(total)
    h_ref[...] = h
    means = jnp.sum(h.reshape(n_blocks, BS, width), axis=1) * (1.0 / BS)
    for i in range(n_blocks // 8):
        p_ref[:, i * width:(i + 1) * width] = means[i * 8:(i + 1) * 8]


def pack_kernel(m_ref, gi_ref, gw_ref, ni_ref, p_ref, params):
    spread, nodes = gi_ref.shape
    params[...] = jnp.zeros_like(params)
    params[:spread, :nodes] = gi_ref[...].astype(F32)
    params[8:8 + spread, :nodes] = gw_ref[...] / jnp.sum(gw_ref[...], axis=0, keepdims=True)
    params[16:16 + ni_ref.shape[0], :nodes] = ni_ref[...].astype(F32)
    tile = params[:8]
    for i in (1, 2):
        tile = tile + pltpu.roll(params[8 * i:8 * i + 8], i * nodes, 1)
    wide = m_ref.shape[1]
    p_ref[:, :wide] = m_ref[...]
    p_ref[:, wide:] = tile


def band_starts(plan):
    band, tile = lax.axis_index("lat"), lax.axis_index("lon")
    starts = []
    for reach, bands in zip(REACHES, plan["bands"]):
        start = band - reach
        if plan["xor"] is not None:
            start = jnp.clip(start, 0, plan["lat"] - bands)
        starts.append(start)
    return band * plan["lon"] + tile, starts


def prepare_kernel(ws_hbm, wn_hbm, wd_hbm, wo_hbm, near_ref, wh_ref, wl_ref, dh_ref, dl_ref, oh_ref, ol_ref, ah_ref, al_ref,
                   w_ref, wd_ref, wo_ref, params, sems):
    width = wd_hbm.shape[0]
    sources, places = [], []
    for layer in range(L):
        sources += [ws_hbm.at[layer], wn_hbm.at[layer]]
        places += [w_ref.at[2 * layer], w_ref.at[2 * layer + 1]]
    copies = fetch(sources + [wd_hbm, wo_hbm], places + [wd_ref, wo_ref], sems)
    rows, nodes = ah_ref.shape
    spread = near_ref.shape[0] // 2
    params[...] = jnp.zeros_like(params)
    params[:spread] = near_ref[:spread]
    params[spread:2 * spread] = near_ref[spread:] / jnp.sum(near_ref[spread:], axis=0, keepdims=True)
    turned = params[...].T
    local, coef = turned[:, :spread], turned[:, spread:2 * spread]
    step = 32
    column = lax.broadcasted_iota(jnp.int32, (step, nodes), 1).astype(F32)
    for at in range(0, rows, step):
        total = jnp.zeros((step, nodes), F32)
        for k in range(spread):
            total = total + jnp.where(column == local[at:at + step, k:k + 1], coef[at:at + step, k:k + 1], 0.0)
        ah_ref[at:at + step], al_ref[at:at + step] = split(total)
    for i in range(2 * L):
        copies[i].wait()
        at = slice((i % 2) * width, (i % 2 + 1) * width)
        wh_ref[i // 2, at], wl_ref[i // 2, at] = split(w_ref[i])
    copies[-2].wait()
    dh_ref[...], dl_ref[...] = split(wd_ref[...])
    copies[-1].wait()
    oh_ref[...], ol_ref[...] = split(wo_ref[...])


def mesh_kernel(plan, *refs):
    n_tables = plan["tables"]
    tables, refs = refs[:n_tables], refs[n_tables:]
    (wh_ref, wl_ref, dh_ref, dl_ref, oh_ref, ol_ref, ah_ref, al_ref, h_ref, t_ref, pred_ref, keep_ref, send_ref,
     th, tl, info, m0f, m0h, m0l, m1f, m1h, m1l, m2h, m2l, xh, xl, pred_buf, sem) = refs
    width = h_ref.shape[1]
    lon, n_blocks, nodes = plan["lon"], plan["blocks"], plan["nodes"]
    k_g2m, k_nbr = plan["k_g2m"], plan["k_nbr"]
    slots = tables[0].shape[0]
    me, (start_b, start0, start1, start2) = band_starts(plan)
    lane = lax.broadcasted_iota(jnp.int32, (8, LANES), 1)
    for c, table in enumerate(tables):
        for i in range(slots):
            if plan["xor"] is None:
                place = i
            else:
                place = me ^ plan["xor"][c * slots + i]
            tile = table[i]
            rows = jnp.concatenate([tile[:, p * width:(p + 1) * width] for p in range(n_blocks // 8)], axis=0)
            at = pl.multiple_of(place * n_blocks, n_blocks)
            th[pl.ds(at, n_blocks), :], tl[pl.ds(at, n_blocks), :] = split(rows)
            info[place] = tile[:, (n_blocks // 8) * width:]

    def band_rows(band, which):
        first = (band - start_b) * lon
        out = []
        for at in range(0, lon, LANES // nodes):
            total = None
            for d in range(min(LANES // nodes, lon - at)):
                value = info[first + at + d]
                if d != which:
                    value = pltpu.roll(value, ((d - which) * nodes) % LANES, 1)
                if total is None:
                    total = value
                else:
                    total = jnp.where(lane >= d * nodes, value, total)
            out.append(total)
        return jnp.concatenate(out, axis=1)

    def near(band, start, bands, per_band):
        three = min(3, bands)
        low = jnp.clip(band - 1, start, start + bands - three)
        at = pl.multiple_of((low - start) * per_band, per_band)
        return pl.ds(at, three * per_band), (low * per_band).astype(F32)

    per_band, per_band_b = lon * nodes, lon * n_blocks

    _, bands0, bands1, bands2 = plan["bands"]
    row_b = lax.broadcasted_iota(jnp.int32, (min(3, plan["bands"][0]) * per_band_b, per_band), 0).astype(F32)
    for i in range(bands0):
        src, base = near(start0 + i, start_b, plan["bands"][0], per_band_b)
        local = band_rows(start0 + i, 0) - base
        coef = band_rows(start0 + i, 1)
        matrix = jnp.zeros(row_b.shape, F32)
        for k in range(k_g2m):
            matrix = matrix + jnp.where(row_b == local[k:k + 1], coef[k:k + 1], 0.0)
        value = dot3(split(matrix.T), (th[src, :], tl[src, :]))
        at = slice(i * per_band, (i + 1) * per_band)
        m0f[at] = value
        m0h[at], m0l[at] = split(value)

    def mixing(layer, src, src_start, src_bands, out, out_start, out_bands):
        srcf, srch, srcl = src
        row = lax.broadcasted_iota(jnp.int32, (LANES, per_band), 0).astype(F32).astype(BF16)
        one, none = jnp.ones((), BF16), jnp.zeros((), BF16)

        def own_rows(i):
            return srcf[pl.ds(pl.multiple_of((out_start + i - src_start) * per_band, per_band), per_band), :]

        for i in range(out_bands):
            band = out_start + i
            rows, base = near(band, src_start, src_bands, per_band)
            local = band_rows(band, 2) - base
            pieces = []
            for at in range(0, min(3, src_bands) * per_band, LANES):
                piece = jnp.zeros(row.shape, BF16)
                here = (local - float(at)).astype(BF16)
                for k in range(k_nbr):
                    piece = piece + jnp.where(row == here[k:k + 1], one, none)
                pieces.append(piece.T)
            matrix = jnp.concatenate(pieces, axis=1)
            agg = (dot(matrix, srch[rows, :]) + dot(matrix, srcl[rows, :])) * (1.0 / k_nbr)
            own = own_rows(i)
            center = own - jnp.mean(own, axis=1, keepdims=True)
            nrm = center * (1.0 / jnp.sqrt(jnp.mean(center * center, axis=1, keepdims=True) + 1e-05))
            at = slice(i * per_band, (i + 1) * per_band)
            xh[at, :width], xl[at, :width] = split(nrm)
            xh[at, width:], xl[at, width:] = split(agg)
        for i in range(out_bands):
            at = slice(i * per_band, (i + 1) * per_band)
            value = own_rows(i) + silu(dot3((xh[at], xl[at]), (wh_ref[layer], wl_ref[layer])))
            if out[0] is not None:
                out[0][at] = value
            out[1][at], out[2][at] = split(value)

    mixing(0, (m0f, m0h, m0l), start0, bands0, (m1f, m1h, m1l), start1, bands1)
    mixing(1, (m1f, m1h, m1l), start1, bands1, (None, m2h, m2l), start2, bands2)

    x = h_ref[...] + dot3((ah_ref[...], al_ref[...]), (m2h[...], m2l[...]))
    z = split(silu(dot3(split(x), (dh_ref[...], dl_ref[...]))))
    pred = dot3(z, (oh_ref[...], ol_ref[...]))
    pred_buf[...] = pred
    out = pltpu.make_async_copy(pred_buf, pred_ref, sem)
    out.start()
    target = t_ref[...]
    resid = pred - target
    err = jnp.sum(resid * resid, axis=0, keepdims=True)
    power = jnp.sum(target * target, axis=0, keepdims=True)
    sums = jnp.concatenate([err, power, jnp.zeros((6, err.shape[1]), F32)], axis=0)
    (zh, zl), (rh, rl) = z, split(resid)

    def dot_t(left, right):
        return lax.dot_general(left, right, (((0,), (0,)), ((), ())), preferred_element_type=F32)

    grad = dot_t(zh, rh) + (dot_t(zh, rl) + dot_t(zl, rh))
    half = width // 2
    swap = second_half(me, plan["half_bits"])
    top, bottom = grad[:half], grad[half:]
    keep_ref[:half] = jnp.where(swap, bottom, top)
    send_ref[:half] = jnp.where(swap, top, bottom)
    keep_ref[half:] = sums
    send_ref[half:] = sums
    out.wait()


def flip(value, mask, count):
    return lax.ppermute(value, AXES, [(i, i ^ mask) for i in range(count)])


def pick(value, at):
    return lax.dynamic_index_in_dim(value, at, 0, keepdims=False)


def gather_all(payload, groups, count, beside):
    table = payload[None]
    for group in groups:
        parts = [table] + [flip(table, m, count) for m in group[1:]]
        if group is groups[-1]:
            parts, beside = lax.optimization_barrier((parts, beside))
        table = jnp.concatenate(parts, axis=0)
    return [table, flip(table, 1, count)], beside


def gather_window(payload, reach):
    tiles = lax.all_gather(payload, "lon")
    n_lat = lax.axis_size("lat")
    bands = []
    for off in range(-reach, reach + 1):
        if off == 0:
            bands.append(tiles)
        else:
            pairs = [(i + off, i) for i in range(n_lat) if 0 <= i + off < n_lat]
            bands.append(lax.ppermute(tiles, "lat", pairs))
    return jnp.concatenate(bands, axis=0)


def shards(
    grid_in,
    target,
    w_enc,
    w_mix_self,
    w_mix_nbr,
    w_dec,
    w_out,
    var_weight,
    g2m_idx,
    g2m_w,
    mesh_nbr,
    m2g_idx,
    m2g_w,
):
    n_lat, n_lon = lax.axis_size("lat"), lax.axis_size("lon")
    count = n_lat * n_lon
    rows, width = grid_in.shape
    n_blocks = rows // BS
    nodes = g2m_idx.shape[0]
    k_g2m, k_nbr = g2m_idx.shape[1], mesh_nbr.shape[1]
    n_var = target.shape[1]
    band, tile = lax.axis_index("lat"), lax.axis_index("lon")
    me = band * n_lon + tile
    butterfly = count & (count - 1) == 0 and n_lat <= 9 and count >= 8
    if butterfly:
        bands = [n_lat] + [min(2 * r + 1, n_lat) for r in REACHES[1:]]
        bits = count.bit_length() - 1
        groups, half_bits = [], [0]
        while bits > 1:
            low = max(1, bits - 2)
            groups.append([(m << low) | (m >> 1) for m in range(1 << (bits - low))])
            half_bits += [low + 1] * (bits - low == 2)
            bits = low
        masks = [0]
        for group in groups:
            masks = [a ^ m for m in group for a in masks]
        masks = masks + [m ^ 1 for m in masks]
    else:
        bands = [2 * r + 1 for r in REACHES]
        masks, half_bits = None, [0]
    plan = dict(
        tables=2 if butterfly else 1, xor=masks, bands=bands, lat=n_lat, lon=n_lon,
        blocks=n_blocks, nodes=nodes, k_g2m=k_g2m, k_nbr=k_nbr, half_bits=half_bits,
    )
    wide = (n_blocks // 8) * width
    h_one, means = pl.pallas_call(
        encode_kernel,
        out_shape=(shape((rows, width)), shape((8, wide))),
        in_specs=[hbm()] * 2,
        out_specs=(vmem(), vmem()),
        scratch_shapes=[
            pltpu.VMEM(grid_in.shape, F32),
            pltpu.VMEM(w_enc.shape, F32),
            pltpu.SemaphoreType.DMA((1 + CHUNKS,)),
        ],
        compiler_params=pltpu.CompilerParams(vmem_limit_bytes=53 * MIB),
        name="encode",
        cost_estimate=pl.CostEstimate(flops=4 * 10**9, bytes_accessed=2 * MIB, transcendentals=0),
    )(grid_in, w_enc)
    payload = pl.pallas_call(
        pack_kernel,
        out_shape=shape((8, wide + LANES)),
        in_specs=[vmem()] * 4,
        out_specs=vmem(),
        scratch_shapes=[pltpu.VMEM((24, LANES), F32)],
        compiler_params=pltpu.CompilerParams(vmem_limit_bytes=4 * MIB),
        name="pack",
    )(means, g2m_idx.T, g2m_w.T, mesh_nbr.T)

    k_m2g = m2g_idx.shape[1]
    local = m2g_idx - band_starts(plan)[1][3] * (n_lon * nodes)
    near = jnp.pad(local.T, ((0, k_m2g), (0, 0))).astype(F32) + jnp.pad(m2g_w.T, ((k_m2g, 0), (0, 0)))
    n2 = bands[3] * n_lon * nodes
    prepared = pl.pallas_call(
        prepare_kernel,
        out_shape=(
            shape((L, 2 * width, width), BF16),
            shape((L, 2 * width, width), BF16),
            shape((width, width), BF16),
            shape((width, width), BF16),
            shape((width, n_var), BF16),
            shape((width, n_var), BF16),
            shape((rows, n2), BF16),
            shape((rows, n2), BF16),
        ),
        in_specs=[hbm()] * 4 + [vmem()],
        out_specs=[vmem()] * 8,
        scratch_shapes=[
            pltpu.VMEM((2 * L, width, width), F32),
            pltpu.VMEM(w_dec.shape, F32),
            pltpu.VMEM(w_out.shape, F32),
            pltpu.VMEM((LANES, rows), F32),
            pltpu.SemaphoreType.DMA((2 * L + 2,)),
        ],
        compiler_params=pltpu.CompilerParams(vmem_limit_bytes=47 * MIB),
        cost_estimate=pl.CostEstimate(flops=0, bytes_accessed=12 * 1024 * 1024, transcendentals=0),
        name="prepare",
    )(w_mix_self, w_mix_nbr, w_dec, w_out, near)

    if butterfly:
        tables, prepared = gather_all(payload, groups, count, prepared)
    else:
        tables = [gather_window(payload, REACHES[0])]
    nb = bands[0] * n_lon * n_blocks
    n0, n1 = (w * n_lon * nodes for w in bands[1:3])
    half = width // 2
    pred, keep, send = pl.pallas_call(
        functools.partial(mesh_kernel, plan),
        out_shape=(shape((rows, n_var)), shape((half + 8, n_var)), shape((half + 8, n_var))),
        in_specs=[vmem()] * (len(tables) + 10),
        out_specs=[hbm(), vmem(), vmem()],
        scratch_shapes=[
            pltpu.VMEM((nb, width), BF16),
            pltpu.VMEM((nb, width), BF16),
            pltpu.VMEM((bands[0] * n_lon, 8, LANES), F32),
            pltpu.VMEM((n0, width), F32),
            pltpu.VMEM((n0, width), BF16),
            pltpu.VMEM((n0, width), BF16),
            pltpu.VMEM((n1, width), F32),
            pltpu.VMEM((n1, width), BF16),
            pltpu.VMEM((n1, width), BF16),
            pltpu.VMEM((n2, width), BF16),
            pltpu.VMEM((n2, width), BF16),
            pltpu.VMEM((n1, 2 * width), BF16),
            pltpu.VMEM((n1, 2 * width), BF16),
            pltpu.VMEM((rows, n_var), F32),
            pltpu.SemaphoreType.DMA(()),
        ],
        compiler_params=pltpu.CompilerParams(vmem_limit_bytes=32 * MIB),
        name="mesh",
    )(*tables, *prepared, h_one, target)

    weights = var_weight.astype(F32)
    wsum = jnp.sum(weights)
    grid_total = rows * count

    def factors(sums):
        scale = sums[1] / grid_total + 1e-06
        return sums[0], weights / (scale * grid_total * wsum)

    if not butterfly:
        swap = second_half(me, half_bits)
        top = jnp.where(swap, send[:half], keep[:half])
        bottom = jnp.where(swap, keep[:half], send[:half])
        total = lax.psum(jnp.concatenate([top, bottom, keep[half:]], axis=0), AXES)
        err, factor = factors(total[width:])
        return (pred, jnp.sum(err * factor), total[:width] * (2.0 * factor)[None, :])

    total = keep + flip(send, 1, count)
    group = groups[-1]
    low = len(group)
    at = (me >> 1) & (low - 1)
    part = half // low
    pieces, sums = total[:half].reshape(low, part, n_var), total[half:]
    total = jnp.concatenate([pick(pieces, at), sums], axis=0)
    for i, received in enumerate(
        [flip(jnp.concatenate([pick(pieces, at ^ i), sums], axis=0), m, count) for i, m in enumerate(group) if m]
    ):
        total = total + received
    for other in groups[-2::-1]:
        received = [flip(total, m, count) for m in other if m]
        for value in received:
            total = total + value
    err, factor = factors(total[part:])
    piece = total[:part] * (2.0 * factor)[None, :]
    pieces = jnp.stack([piece] + [flip(piece, m, count) for m in group if m])
    own = jnp.concatenate([pick(pieces, at ^ i) for i in range(low)], axis=0)
    other = flip(own, 1, count)
    swap = second_half(me, half_bits)
    grad_out = jnp.concatenate([jnp.where(swap, other, own), jnp.where(swap, own, other)], axis=0)
    return (pred, jnp.sum(err * factor), grad_out)


def solution(mesh):
    placed = (
        P(AXES, None),
        P(AXES, None),
        P(),
        P(),
        P(),
        P(),
        P(),
        P(),
        P(AXES, None),
        P(AXES, None),
        P(AXES, None),
        P(AXES, None),
        P(AXES, None),
    )
    return jax.shard_map(
        shards,
        mesh=mesh,
        in_specs=placed,
        out_specs=(P(AXES, None), P(), P()),
        check_vma=False,
    )
```
